32 devices in a mesh: grp: 2 (over y), src: 4 (over z), rcv: 4 (over x, core).
Axes of the slice: x: 2, y: 2, z: 4, core: 2. Of those that a mesh axis runs over, the one named last changes fastest.
Arguments:
- traces: bfloat16 [8, 1024, 2048], P(None, ('grp', 'rcv', 'src')), parts along dimension 1, may hold values from -120 to 120
- alive: int32 [8, 1024], P(None, ('grp', 'rcv', 'src')), parts along dimension 1, may hold values 0 or 1
- picks: int32 [32, 32], P(('grp', 'rcv', 'src')), parts along dimension 0, may hold values from 0 to 31, each once within a row
Outputs:
- correlations: bfloat16 [65, 256, 512], P(None, ('grp', 'src'), 'rcv'), parts along dimension 1
The draws below stay inside these ranges and needn't reach their ends.
There are 2 independent parts, one for each index of `grp`. The reference program is written for one: setup_inputs(seed, part) draws one part's arguments, and reference() takes and returns one part's arrays. A program takes and returns all parts, laid end to end along the dimension named above; each array names one. Nothing has to cross between parts.
Inputs may be any that keep to these rules, and one draw needn't show every extreme that they name: `picks`: row b belongs to the channel block of 32 channels numbered b along rcv+src (rcv the slower); it orders that block's channels, and its first 8 entries name the block's virtual sources.
All inputs are finite; a program needn't handle non-finite values. No bound on the sum of `alive` on one device may be relied on, other than what follows from the above.
Results may differ from the reference program's by a relative error of at most 0.0056.
Values may be sent and summed in bfloat16 or wider, within the bound.
A program may use at most 64 MiB of HBM per device.

```python
import math
import jax
import jax.numpy as jnp
from jax import lax

SEGS = 8
SAMPLES = 2048
BINS = 256
LOWBIN = 16
MAXLAG = 32
LAGS = 65
RCV_DEV = 128
CH_DEV = 32
PICK = 8
SOURCES = 128
CHANNELS = 512
N_SRC = 4
N_RCV = 4


def draw_traces(key, part):
    key_base, key_chan, key_env = jax.random.split(key, 3)
    shape = (SEGS, CHANNELS, SAMPLES)
    base = jnp.clip(jax.random.normal(key_base, shape, jnp.float32), -4.0, 4.0)
    chan_scale = jnp.exp(jax.random.uniform(key_chan, (1, CHANNELS, 1), jnp.float32, 0.0, math.log(10.0)))
    envelope = jnp.exp(jax.random.uniform(key_env, shape, jnp.float32, 0.0, math.log(10.0)))
    return (0.2 * base * chan_scale * envelope).astype(jnp.bfloat16)


def with_ends(entries, stream_key, low, high):
    place = [jax.random.randint(jax.random.fold_in(stream_key, axis), (), 0, length) for axis, length in enumerate(entries.shape)]
    longest = entries.shape.index(max(entries.shape))
    neighbour = place[:longest] + [(place[longest] + 1) % entries.shape[longest]] + place[longest + 1:]
    return entries.at[tuple(place)].set(low).at[tuple(neighbour)].set(high)


def setup_inputs(seed: int = 0, part: int = 0) -> dict:
    streams_of = jax.random.split(jax.random.key(seed), 4)
    part_keys = jax.random.split(jax.random.fold_in(streams_of[3], part), 4)
    traces = draw_traces(jax.random.fold_in(jax.random.fold_in(streams_of[3], part), 71), part)
    alive = with_ends((jax.random.randint(part_keys[1], (SEGS, CHANNELS), 0, 8) < 7).astype(jnp.int32), jax.random.fold_in(part_keys[1], 1), 0, 1)
    picks = jax.vmap(lambda own: jax.random.permutation(own, CH_DEV))(jax.random.split(part_keys[2], (N_RCV * N_SRC))).reshape((N_RCV * N_SRC, CH_DEV)).astype(jnp.int32)
    return {"traces": traces, "alive": alive, "picks": picks}


def dft_table():
    sample_ids = jnp.arange(SAMPLES, dtype=jnp.int32)
    bin_ids = LOWBIN + jnp.arange(BINS, dtype=jnp.int32)
    angles = jnp.mod(sample_ids[:, None] * bin_ids[None, :], SAMPLES).astype(jnp.float32) * (2.0 * math.pi / SAMPLES)
    hann_taper = 0.5 - 0.5 * jnp.cos(sample_ids.astype(jnp.float32) * (2.0 * math.pi / SAMPLES))
    joined = jnp.concatenate([hann_taper[:, None] * jnp.cos(angles), -hann_taper[:, None] * jnp.sin(angles)], axis=1)
    return joined.astype(jnp.bfloat16)

def lag_tables():
    shifts = jnp.arange(LAGS, dtype=jnp.int32) - MAXLAG
    bin_ids = LOWBIN + jnp.arange(BINS, dtype=jnp.int32)
    angles = jnp.mod(shifts[:, None] * bin_ids[None, :], SAMPLES).astype(jnp.float32) * (2.0 * math.pi / SAMPLES)
    lag_scale = 1.0 / math.sqrt(SEGS * BINS)
    return (lag_scale * jnp.cos(angles), -lag_scale * jnp.sin(angles))

def spectra(samples, live, transform):
    seg_count, row_count = (samples.shape[0], samples.shape[1])
    raw_spec = jnp.dot(samples.reshape(seg_count * row_count, SAMPLES), transform, preferred_element_type=jnp.float32)
    mean_square = lax.optimization_barrier(jnp.mean(jnp.square(samples.astype(jnp.float32)), axis=-1)).reshape(seg_count * row_count, 1)
    weight = live.reshape(seg_count * row_count, 1).astype(jnp.float32) / jnp.sqrt(SAMPLES * (mean_square + 1e-06))
    return (raw_spec * weight).reshape(seg_count, row_count, 2 * BINS).astype(jnp.bfloat16)

def correlate(sources, receivers, cosine_lag_table, sine_lag_table):
    seg_count, src_count = (sources.shape[0], sources.shape[1])
    receiver_count = receivers.shape[1]
    source_block_view = sources.reshape(seg_count, src_count, 2, BINS).transpose(3, 1, 0, 2).reshape(BINS, src_count, 2 * seg_count)
    receiver_view = receivers.reshape(seg_count, receiver_count, 2, BINS)
    real_part = receiver_view[:, :, 0, :]
    imag_part = receiver_view[:, :, 1, :]
    real_cols = jnp.stack([real_part, imag_part], axis=1)
    imag_cols = jnp.stack([-imag_part, real_part], axis=1)
    column_entries = jnp.concatenate([real_cols, imag_cols], axis=2).transpose(3, 0, 1, 2).reshape(BINS, 2 * seg_count, 2 * receiver_count)
    spectral_sum_total = jnp.einsum('cni,cip->cnp', source_block_view.astype(jnp.float32), column_entries.astype(jnp.float32))
    summed_result = jnp.einsum('iy,yhp->ihp', cosine_lag_table, spectral_sum_total[:, :, :receiver_count], precision=lax.Precision.HIGHEST)
    summed_result = summed_result + jnp.einsum('iy,yhp->ihp', sine_lag_table, spectral_sum_total[:, :, receiver_count:], precision=lax.Precision.HIGHEST)
    return summed_result

def reference(traces, alive, picks):
    transform = dft_table()
    cosine_lag_table, sine_lag_table = lag_tables()
    local_spec = spectra(traces, alive, transform)
    chosen = picks[:, :PICK].reshape(N_RCV, N_SRC, PICK)
    block_ids = (jnp.arange(N_RCV, dtype=jnp.int32)[:, None] * N_SRC + jnp.arange(N_SRC, dtype=jnp.int32)[None, :]) * CH_DEV
    source_channels = (block_ids[:, :, None] + chosen).transpose(1, 0, 2).reshape(SOURCES).astype(jnp.int32)
    sources = jnp.take(local_spec, source_channels, axis=1)
    panels = local_spec.reshape(SEGS, N_RCV, RCV_DEV, 2 * BINS).transpose(1, 0, 2, 3)
    results = lax.map(lambda panel: correlate(sources, panel, cosine_lag_table, sine_lag_table), panels)
    joined = results.transpose(1, 2, 0, 3).reshape(LAGS, SOURCES, CHANNELS)
    return joined.astype(jnp.bfloat16)
```

```python
import functools
import math

import jax
import jax.numpy as jnp
import numpy as np
from jax import lax
from jax.experimental import pallas as pl
from jax.experimental.pallas import tpu as pltpu
from jax.sharding import PartitionSpec as P

BINS = 256
LOWBIN = 16
MAXLAG = 32
LAGS = 2 * MAXLAG + 1
SRC_DEV = 32
SEGS_PER_CHUNK = 2
MESH = pl.DeviceIdType.MESH


def dft_table(samples):
    t = np.arange(samples)
    k = LOWBIN + np.arange(BINS)
    angles = ((t[:, None] * k[None, :]) % samples) * (2.0 * math.pi / samples)
    taper = (0.5 - 0.5 * np.cos(t * (2.0 * math.pi / samples)))[:, None]
    joined = np.concatenate([taper * np.cos(angles), -taper * np.sin(angles)], axis=1)
    return joined.astype(np.float32).astype(jnp.bfloat16)


def lag_tables(samples):
    tau = np.arange(MAXLAG + 1)
    k = LOWBIN + np.arange(BINS)
    angles = ((tau[:, None] * k[None, :]) % samples) * (2.0 * math.pi / samples)
    scale = 1.0 / math.sqrt(samples)
    cosine, sine = scale * np.cos(angles), -scale * np.sin(angles)
    even = np.concatenate([cosine, cosine], axis=1)
    odd = np.concatenate([sine, -sine], axis=1)
    return even.astype(np.float32), odd.astype(np.float32)


def selectors(segs, channels, picked, n_rcv):
    rows = segs * picked
    entry = np.zeros((rows, channels), np.float32)
    entry[np.arange(rows), np.arange(rows) % picked] = 1.0
    column = np.arange(segs * channels)[None, :] - (np.arange(rows) // picked)[:, None] * channels
    order = np.zeros((segs, n_rcv, picked, n_rcv, segs, picked), np.float32)
    for g in range(segs):
        for r in range(n_rcv):
            for j in range(picked):
                order[g, r, j, r, g, j] = 1.0
    total = rows * n_rcv
    return entry, column.astype(np.float32), order.reshape(total, total).astype(jnp.bfloat16)


def kernel(
    segs, n_src, n_rcv,
    traces, alive, picks, table, even, odd, entry, column, order, out,
    panel, sources, phased, total,
    right_send, right_recv, left_send, left_recv, src_send, src_recv,
):
    channels = traces.shape[0] // segs
    samples = traces.shape[1]
    width = table.shape[1]
    chunk_rows = SEGS_PER_CHUNK * channels
    chunks = segs // SEGS_PER_CHUNK
    me, ring = lax.axis_index("src"), lax.axis_index("rcv")
    lines = ((1, right_send, right_recv), (-1, left_send, left_recv))

    barrier = pltpu.get_barrier_semaphore()
    for step, _, _ in lines:
        @pl.when((me + step >= 0) & (me + step < n_src))
        def _(step=step):
            pl.semaphore_signal(barrier, inc=1, device_id={"src": me + step}, device_id_type=MESH)
    for d in range(1, n_rcv):
        pl.semaphore_signal(
            barrier, inc=1, device_id={"rcv": lax.rem(ring + d, n_rcv)}, device_id_type=MESH
        )

    def hop(step, send, recv, h, q, shard):
        rows = pl.ds(q * chunk_rows, chunk_rows)
        return pltpu.make_async_remote_copy(
            src_ref=panel.at[shard, rows], dst_ref=panel.at[shard, rows],
            send_sem=send.at[h, q], recv_sem=recv.at[h, q],
            device_id={"src": me + step}, device_id_type=MESH,
        )

    def on_sent(h, q, act):
        for step, send, recv in lines:
            shard, target = me - step * h, me + step

            @pl.when((shard >= 0) & (shard < n_src) & (target >= 0) & (target < n_src))
            def _(step=step, send=send, recv=recv, shard=shard):
                act(hop(step, send, recv, h, q, shard))

    def arrived(h, q):
        for step, send, recv in lines:
            shard = me - step * (h + 1)

            @pl.when((shard >= 0) & (shard < n_src))
            def _(step=step, send=send, recv=recv, shard=shard):
                hop(step, send, recv, h, q, shard).wait_recv()

    def swap(d, owner):
        return pltpu.make_async_remote_copy(
            src_ref=sources.at[owner], dst_ref=sources.at[owner],
            send_sem=src_send.at[d - 1], recv_sem=src_recv.at[d - 1],
            device_id={"rcv": lax.rem(ring + d, n_rcv)}, device_id_type=MESH,
        )

    diagonal = lax.broadcasted_iota(jnp.int32, (channels, channels), 0) == lax.broadcasted_iota(
        jnp.int32, (channels, channels), 1
    )
    live = jnp.concatenate(
        [
            jnp.sum(
                jnp.where(diagonal, alive[g : g + 1, :].astype(jnp.float32), 0.0),
                axis=1, keepdims=True,
            )
            for g in range(segs)
        ],
        axis=0,
    )
    for q in range(chunks):
        rows = slice(q * chunk_rows, (q + 1) * chunk_rows)
        block = traces[rows, :]
        raw = jnp.dot(block, table[...], preferred_element_type=jnp.float32)
        wide = block.astype(jnp.float32)
        mean_square = jnp.mean(wide * wide, axis=1, keepdims=True)
        weight = live[rows] / jnp.sqrt(samples * (mean_square + 1e-06))
        panel[me, rows, :] = (raw * weight).astype(jnp.bfloat16)
        if q == 0:
            neighbours = (me > 0).astype(jnp.int32) + (me < n_src - 1).astype(jnp.int32)
            pl.semaphore_wait(barrier, n_rcv - 1 + neighbours)
        on_sent(0, q, lambda copy: copy.start())

    chosen = jnp.sum(entry[...] * picks[...].astype(jnp.float32), axis=1, keepdims=True)
    one_hot = jnp.where(column[...] == chosen, 1.0, 0.0).astype(jnp.bfloat16)
    sources[ring] = jnp.dot(one_hot, panel[me], preferred_element_type=jnp.float32).astype(
        jnp.bfloat16
    )
    for d in range(1, n_rcv):
        swap(d, ring).start()
    for d in range(1, n_rcv):
        swap(d, lax.rem(ring - d + n_rcv, n_rcv)).wait_recv()
    ordered = jnp.dot(
        order[...], sources[...].reshape(order.shape[1], width), preferred_element_type=jnp.float32
    )

    base = (MAXLAG + 1) * SRC_DEV
    half = width // 2
    for q in range(chunks):
        for i in range(SEGS_PER_CHUNK):
            g = q * SEGS_PER_CHUNK + i
            block = ordered[g * SRC_DEV : (g + 1) * SRC_DEV]
            turned = jnp.concatenate([block[:, half:], block[:, :half]], axis=1)
            lanes = slice(i * width, (i + 1) * width)
            for lag in range(MAXLAG + 1):
                at = slice(lag * SRC_DEV, (lag + 1) * SRC_DEV)
                phased[q, at, lanes] = (block * even[lag : lag + 1, :]).astype(jnp.bfloat16)
            for lag in range(1, MAXLAG + 1):
                at = slice(base + (lag - 1) * SRC_DEV, base + lag * SRC_DEV)
                phased[q, at, lanes] = (turned * odd[lag : lag + 1, :]).astype(jnp.bfloat16)
        if n_src > 2:
            arrived(0, q)
            on_sent(1, q, lambda copy: copy.start())
    for h in range(1, n_src - 2):
        for q in range(chunks):
            arrived(h, q)
            on_sent(h + 1, q, lambda copy: copy.start())

    def receivers(q, i):
        if channels % 16 == 0:
            at = q * chunk_rows + i * channels
            return panel[:, at : at + channels, :].reshape(n_src * channels, width)
        block = panel[:, q * chunk_rows : (q + 1) * chunk_rows, :].astype(jnp.float32)
        block = block.reshape(n_src, SEGS_PER_CHUNK, channels, width)[:, i]
        return block.reshape(n_src * channels, width).astype(jnp.bfloat16)

    height = total.shape[0]
    part = height // 5
    for q in range(chunks):
        arrived(n_src - 2, q)
        columns = jnp.concatenate([receivers(q, i) for i in range(SEGS_PER_CHUNK)], axis=1)
        for p in range(height // part):
            at = slice(p * part, (p + 1) * part)
            product = lax.dot_general(
                phased[q, at, :], columns, (((1,), (1,)), ((), ())),
                preferred_element_type=jnp.float32,
            )
            total[at, :] = product if q == 0 else total[at, :] + product

    out[MAXLAG] = total[:SRC_DEV, :].astype(out.dtype)
    for lag in range(1, MAXLAG + 1):
        symmetric = total[lag * SRC_DEV : (lag + 1) * SRC_DEV, :]
        skew = total[base + (lag - 1) * SRC_DEV : base + lag * SRC_DEV, :]
        out[MAXLAG + lag] = (symmetric + skew).astype(out.dtype)
        out[MAXLAG - lag] = (symmetric - skew).astype(out.dtype)

    for h in range(n_src - 1):
        for q in range(chunks):
            on_sent(h, q, lambda copy: copy.wait_send())
    for d in range(1, n_rcv):
        swap(d, ring).wait_send()


def shards(traces, alive, picks):
    segs, channels, samples = traces.shape
    n_src, n_rcv = lax.axis_size("src"), lax.axis_size("rcv")
    picked = SRC_DEV // n_rcv
    chunks = segs // SEGS_PER_CHUNK
    table = dft_table(samples)
    even, odd = lag_tables(samples)
    entry, column, order = selectors(segs, channels, picked, n_rcv)
    width = 2 * BINS
    vmem = pl.BlockSpec(memory_space=pltpu.VMEM)
    dma = pltpu.SemaphoreType.DMA
    return pl.pallas_call(
        functools.partial(kernel, segs, n_src, n_rcv),
        out_shape=jax.ShapeDtypeStruct((LAGS, SRC_DEV, n_src * channels), jnp.bfloat16),
        in_specs=[vmem] * 9,
        out_specs=vmem,
        scratch_shapes=[
            pltpu.VMEM((n_src, segs * channels, width), jnp.bfloat16),
            pltpu.VMEM((n_rcv, segs * picked, width), jnp.bfloat16),
            pltpu.VMEM((chunks, LAGS * SRC_DEV, SEGS_PER_CHUNK * width), jnp.bfloat16),
            pltpu.VMEM((LAGS * SRC_DEV, n_src * channels), jnp.float32),
            dma((n_src - 1, chunks)), dma((n_src - 1, chunks)),
            dma((n_src - 1, chunks)), dma((n_src - 1, chunks)),
            dma((n_rcv - 1,)), dma((n_rcv - 1,)),
        ],
        compiler_params=pltpu.CompilerParams(
            collective_id=0, has_side_effects=True, vmem_limit_bytes=48 * 1024 * 1024
        ),
        cost_estimate=pl.CostEstimate(flops=3 * 10**9, bytes_accessed=5 * 10**6, transcendentals=0),
    )(
        traces.reshape(segs * channels, samples), alive, picks,
        jnp.asarray(table), jnp.asarray(even), jnp.asarray(odd),
        jnp.asarray(entry), jnp.asarray(column), jnp.asarray(order),
    )


def solution(mesh):
    return jax.shard_map(
        shards,
        mesh=mesh,
        in_specs=(
            P(None, ("grp", "rcv", "src"), None),
            P(None, ("grp", "rcv", "src")),
            P(("grp", "rcv", "src"), None),
        ),
        out_specs=P(None, ("grp", "src"), "rcv"),
        check_vma=False,
    )
```

```python
import functools
import math

import jax
import jax.numpy as jnp
import numpy as np
from jax import lax
from jax.experimental import pallas as pl
from jax.experimental.pallas import tpu as pltpu
from jax.sharding import PartitionSpec as P

BINS = 256
LOWBIN = 16
MAXLAG = 32
LAGS = 2 * MAXLAG + 1
SRC_DEV = 32
MESH = pl.DeviceIdType.MESH


def dft_table(samples):
    t = np.arange(samples)
    k = LOWBIN + np.arange(BINS)
    angles = ((t[:, None] * k[None, :]) % samples) * (2.0 * math.pi / samples)
    taper = (0.5 - 0.5 * np.cos(t * (2.0 * math.pi / samples)))[:, None]
    joined = np.concatenate([taper * np.cos(angles), -taper * np.sin(angles)], axis=1)
    return joined.astype(np.float32).astype(jnp.bfloat16)


def lag_tables(samples):
    tau = np.arange(MAXLAG + 1)
    k = LOWBIN + np.arange(BINS)
    angles = ((tau[:, None] * k[None, :]) % samples) * (2.0 * math.pi / samples)
    scale = 1.0 / math.sqrt(samples)
    cosine, sine = scale * np.cos(angles), -scale * np.sin(angles)
    even = np.concatenate([cosine, cosine], axis=1)
    odd = np.concatenate([sine, -sine], axis=1)
    return even.astype(np.float32), odd.astype(np.float32)


def selectors(segs, channels, picked, n_rcv):
    rows = segs * picked
    entry = np.zeros((rows, channels), np.float32)
    entry[np.arange(rows), np.arange(rows) % picked] = 1.0
    column = np.arange(segs * channels)[None, :] - (np.arange(rows) // picked)[:, None] * channels
    order = np.zeros((segs, n_rcv, picked, n_rcv, segs, picked), np.float32)
    for g in range(segs):
        for r in range(n_rcv):
            for j in range(picked):
                order[g, r, j, r, g, j] = 1.0
    total = rows * n_rcv
    return entry, column.astype(np.float32), order.reshape(total, total).astype(jnp.bfloat16)


def kernel(
    segs, n_src, n_rcv, per_chunk,
    traces_hbm, alive_hbm, picks_hbm, table_hbm, even_hbm, odd_hbm, entry_hbm, column_hbm, order_hbm,
    out,
    traces, alive, picks, table, even, odd, entry, column, order,
    panel, sources, phased, total,
    right_send, right_recv, left_send, left_recv, src_send, src_recv, load_sem,
):
    channels = traces.shape[0] // segs
    samples = traces.shape[1]
    width = table.shape[1]
    chunk_rows = per_chunk * channels
    chunks = segs // per_chunk
    first = segs * channels // 4
    middle = samples // 2
    pairs = (
        (traces_hbm.at[pl.ds(0, first)], traces.at[pl.ds(0, first)]),
        (table_hbm.at[pl.ds(0, middle)], table.at[pl.ds(0, middle)]),
        (table_hbm.at[pl.ds(middle, middle)], table.at[pl.ds(middle, middle)]),
        (alive_hbm, alive),
        (traces_hbm.at[pl.ds(first, 3 * first)], traces.at[pl.ds(first, 3 * first)]),
        (picks_hbm, picks), (entry_hbm, entry), (column_hbm, column), (order_hbm, order),
        (even_hbm, even), (odd_hbm, odd),
    )
    loads = [pltpu.make_async_copy(a, b, load_sem.at[i]) for i, (a, b) in enumerate(pairs)]
    for load in loads:
        load.start()
    me, ring = lax.axis_index("src"), lax.axis_index("rcv")
    lines = ((1, right_send, right_recv), (-1, left_send, left_recv))

    barrier = pltpu.get_barrier_semaphore()
    for step, _, _ in lines:
        @pl.when((me + step >= 0) & (me + step < n_src))
        def _(step=step):
            pl.semaphore_signal(barrier, inc=1, device_id={"src": me + step}, device_id_type=MESH)
    for d in range(1, n_rcv):
        pl.semaphore_signal(
            barrier, inc=1, device_id={"rcv": lax.rem(ring + d, n_rcv)}, device_id_type=MESH
        )

    def hop(step, send, recv, h, q, shard):
        rows = pl.ds(q * chunk_rows, chunk_rows)
        return pltpu.make_async_remote_copy(
            src_ref=panel.at[shard, rows], dst_ref=panel.at[shard, rows],
            send_sem=send.at[h, q], recv_sem=recv.at[h, q],
            device_id={"src": me + step}, device_id_type=MESH,
        )

    def on_sent(h, q, act):
        for step, send, recv in lines:
            shard, target = me - step * h, me + step

            @pl.when((shard >= 0) & (shard < n_src) & (target >= 0) & (target < n_src))
            def _(step=step, send=send, recv=recv, shard=shard):
                act(hop(step, send, recv, h, q, shard))

    def arrived(h, q):
        for step, send, recv in lines:
            shard = me - step * (h + 1)

            @pl.when((shard >= 0) & (shard < n_src))
            def _(step=step, send=send, recv=recv, shard=shard):
                hop(step, send, recv, h, q, shard).wait_recv()

    def swap(d, owner):
        return pltpu.make_async_remote_copy(
            src_ref=sources.at[owner], dst_ref=sources.at[owner],
            send_sem=src_send.at[d - 1], recv_sem=src_recv.at[d - 1],
            device_id={"rcv": lax.rem(ring + d, n_rcv)}, device_id_type=MESH,
        )

    diagonal = lax.broadcasted_iota(jnp.int32, (channels, channels), 0) == lax.broadcasted_iota(
        jnp.int32, (channels, channels), 1
    )
    def spectrum(start, stop):
        rows = slice(start, stop)
        block = traces[rows, :]
        raw = jnp.dot(block[:, :middle], table[:middle, :], preferred_element_type=jnp.float32)
        if start == 0:
            loads[2].wait()
        raw = raw + jnp.dot(
            block[:, middle:], table[middle:, :], preferred_element_type=jnp.float32
        )
        wide = block.astype(jnp.float32)
        mean_square = jnp.mean(wide * wide, axis=1, keepdims=True)
        if start == 0:
            loads[3].wait()
        live = jnp.concatenate(
            [
                jnp.sum(
                    jnp.where(diagonal, alive[g : g + 1, :].astype(jnp.float32), 0.0),
                    axis=1, keepdims=True,
                )
                for g in range(start // channels, stop // channels)
            ],
            axis=0,
        )
        weight = live / jnp.sqrt(samples * (mean_square + 1e-06))
        panel[me, rows, :] = (raw * weight).astype(jnp.bfloat16)

    loads[0].wait()
    loads[1].wait()
    spectrum(0, first)
    neighbours = (me > 0).astype(jnp.int32) + (me < n_src - 1).astype(jnp.int32)
    pl.semaphore_wait(barrier, n_rcv - 1 + neighbours)
    for q in range(chunks // 4):
        on_sent(0, q, lambda copy: copy.start())
    loads[4].wait()
    spectrum(first, 4 * first)
    for q in range(chunks // 4, chunks):
        on_sent(0, q, lambda copy: copy.start())

    for load in loads[5:]:
        load.wait()
    chosen = jnp.sum(entry[...] * picks[...].astype(jnp.float32), axis=1, keepdims=True)
    one_hot = jnp.where(column[...] == chosen, 1.0, 0.0).astype(jnp.bfloat16)
    sources[ring] = jnp.dot(one_hot, panel[me], preferred_element_type=jnp.float32).astype(
        jnp.bfloat16
    )
    for d in range(1, n_rcv):
        swap(d, ring).start()
    for d in range(1, n_rcv):
        swap(d, lax.rem(ring - d + n_rcv, n_rcv)).wait_recv()
    ordered = jnp.dot(
        order[...], sources[...].reshape(order.shape[1], width), preferred_element_type=jnp.float32
    )

    base = (MAXLAG + 1) * SRC_DEV
    half = width // 2
    for q in range(chunks):
        for g in range(q * per_chunk, (q + 1) * per_chunk):
            block = ordered[g * SRC_DEV : (g + 1) * SRC_DEV]
            turned = jnp.concatenate([block[:, half:], block[:, :half]], axis=1)
            lanes = slice(g * width, (g + 1) * width)
            for lag in range(MAXLAG + 1):
                at = slice(lag * SRC_DEV, (lag + 1) * SRC_DEV)
                phased[at, lanes] = (block * even[lag : lag + 1, :]).astype(jnp.bfloat16)
            for lag in range(1, MAXLAG + 1):
                at = slice(base + (lag - 1) * SRC_DEV, base + lag * SRC_DEV)
                phased[at, lanes] = (turned * odd[lag : lag + 1, :]).astype(jnp.bfloat16)
        if n_src > 2:
            arrived(0, q)
            on_sent(1, q, lambda copy: copy.start())
    for h in range(1, n_src - 2):
        for q in range(chunks):
            arrived(h, q)
            on_sent(h + 1, q, lambda copy: copy.start())

    def receivers(g):
        if channels % 16 == 0:
            return panel[:, g * channels : (g + 1) * channels, :].reshape(n_src * channels, width)
        q, i = g // per_chunk, g % per_chunk
        block = panel[:, q * chunk_rows : (q + 1) * chunk_rows, :].astype(jnp.float32)
        block = block.reshape(n_src, per_chunk, channels, width)[:, i]
        return block.reshape(n_src * channels, width).astype(jnp.bfloat16)

    def product(rows, g0, columns):
        return lax.dot_general(
            phased[rows, g0 * width : g0 * width + columns.shape[1]], columns,
            (((1,), (1,)), ((), ())), preferred_element_type=jnp.float32,
        )

    part = total.shape[0] // 5
    g0 = 0
    for q in range(chunks):
        arrived(n_src - 2, q)
        g1 = (q + 1) * per_chunk
        if g1 - g0 < 2 and q < chunks - 2:
            continue
        columns = jnp.concatenate([receivers(g) for g in range(g0, g1)], axis=1)
        if q < chunks - 1:
            for p in range(5):
                at = slice(p * part, (p + 1) * part)
                value = product(at, g0, columns)
                total[at, :] = value if g0 == 0 else total[at, :] + value
            g0 = g1

    group = MAXLAG // 4
    for p in range(4):
        lag0 = 0 if p == 0 else 1 + p * group
        even_at = slice(lag0 * SRC_DEV, (1 + (p + 1) * group) * SRC_DEV)
        odd_at = slice(base + p * group * SRC_DEV, base + (p + 1) * group * SRC_DEV)
        symmetric = total[even_at, :] + product(even_at, g0, columns)
        skew = total[odd_at, :] + product(odd_at, g0, columns)
        for lag in range(lag0, 1 + (p + 1) * group):
            i = lag - lag0
            e = symmetric[i * SRC_DEV : (i + 1) * SRC_DEV]
            if lag == 0:
                out[MAXLAG] = e.astype(out.dtype)
                continue
            i = lag - 1 - p * group
            o = skew[i * SRC_DEV : (i + 1) * SRC_DEV]
            out[MAXLAG + lag] = (e + o).astype(out.dtype)
            out[MAXLAG - lag] = (e - o).astype(out.dtype)

    for h in range(n_src - 1):
        for q in range(chunks):
            on_sent(h, q, lambda copy: copy.wait_send())
    for d in range(1, n_rcv):
        swap(d, ring).wait_send()


def shards(traces, alive, picks):
    segs, channels, samples = traces.shape
    n_src, n_rcv = lax.axis_size("src"), lax.axis_size("rcv")
    picked = SRC_DEV // n_rcv
    per_chunk = max(1, 16 // channels)
    chunks = segs // per_chunk
    table = dft_table(samples)
    even, odd = lag_tables(samples)
    entry, column, order = selectors(segs, channels, picked, n_rcv)
    width = 2 * BINS
    vmem = pl.BlockSpec(memory_space=pltpu.VMEM)
    dma = pltpu.SemaphoreType.DMA
    operands = (
        traces.reshape(segs * channels, samples), alive, picks,
        jnp.asarray(table), jnp.asarray(even), jnp.asarray(odd),
        jnp.asarray(entry), jnp.asarray(column), jnp.asarray(order),
    )
    return pl.pallas_call(
        functools.partial(kernel, segs, n_src, n_rcv, per_chunk),
        out_shape=jax.ShapeDtypeStruct((LAGS, SRC_DEV, n_src * channels), jnp.bfloat16),
        in_specs=[pl.BlockSpec(memory_space=pltpu.HBM)] * len(operands),
        out_specs=vmem,
        scratch_shapes=[pltpu.VMEM(a.shape, a.dtype) for a in operands]
        + [
            pltpu.VMEM((n_src, segs * channels, width), jnp.bfloat16),
            pltpu.VMEM((n_rcv, segs * picked, width), jnp.bfloat16),
            pltpu.VMEM((LAGS * SRC_DEV, segs * width), jnp.bfloat16),
            pltpu.VMEM((LAGS * SRC_DEV, n_src * channels), jnp.float32),
            dma((n_src - 1, chunks)), dma((n_src - 1, chunks)),
            dma((n_src - 1, chunks)), dma((n_src - 1, chunks)),
            dma((n_rcv - 1,)), dma((n_rcv - 1,)), dma((len(operands) + 2,)),
        ],
        compiler_params=pltpu.CompilerParams(
            collective_id=0, has_side_effects=True, vmem_limit_bytes=60 * 1024 * 1024
        ),
        cost_estimate=pl.CostEstimate(flops=3 * 10**9, bytes_accessed=5 * 10**6, transcendentals=0),
    )(*operands)


def solution(mesh):
    return jax.shard_map(
        shards,
        mesh=mesh,
        in_specs=(
            P(None, ("grp", "rcv", "src"), None),
            P(None, ("grp", "rcv", "src")),
            P(("grp", "rcv", "src"), None),
        ),
        out_specs=P(None, ("grp", "src"), "rcv"),
        check_vma=False,
    )
```
